32 devices in a mesh: tile: 16 (over z, y, core), sun: 2 (over x).
Axes of the slice: x: 2, y: 2, z: 4, core: 2. Of those that a mesh axis runs over, the one named last changes fastest.
Arguments:
- heights: float32 [2048, 1024], P('tile', 'sun'), may hold values from 0 to 31.5, as said below
- classes: int32 [2048, 1024], P('tile', 'sun'), may hold values from 0 to 15
- rate_table: float32 [2, 16], replicated, may hold values from 0.03 to 0.24
- anomaly: float32 [2, 2048, 1024], P(None, 'tile', 'sun'), may hold values from -16 to 16
- view_coef: bfloat16 [3, 2048, 1024], P(None, 'tile', 'sun'), may hold values from 0.099609375 to 0.8984375
- sun_geometry: int32 [2, 4], P('sun'), may hold values from -1 to 24
- sun_radiation: float32 [2, 3], P('sun'), may hold values from 50 to 900, as said below
- record_tile: int32 [32768, 1], P(('tile', 'sun')), may hold values from 0 to 15; in each aligned block of 1024 rows (0 to 1023, 1024 to 2047, ...) at most 128 rows name the same one
- record_cell: int32 [32768], P(('tile', 'sun')), may hold values from 0 to 131071
- record_air: float32 [32768], P(('tile', 'sun')), may hold values from 20 to 35
Outputs:
- radiant_temp: float32 [2, 2048, 1024], P('sun', 'tile')
- record_excess: float32 [32768], P(('tile', 'sun'))
The draws below stay inside these ranges and needn't reach their ends.
Inputs may be any that keep to these rules, and one draw needn't show every extreme that they name: `heights`: terrain on every cell; buildings and trees stand on scattered cells. `sun_radiation`: columns lie in 100 to 900, 50 to 250 and 300 to 420. `record_tile`: among the records of one device at most 128 name one tile, and in every draw some tile is named 128 times by one device.
All inputs are finite; a program needn't handle non-finite values.
Results may differ from the reference program's by a relative error of at most 0.0003.
Values sent between devices are 32-bit elements; how exact they have to be, the bound alone decides.
A program may use at most 64 MiB of HBM per device.

```python
import math
import jax
import jax.numpy as jnp
import numpy as np
from jax import lax

TR = 128
MAXSTEP = 24
HEAT_STEPS = 4
CLASSES = 16
REC_DEV = 1024
NTILE = 16
SUNS = 2
CAP = 128
NY = 2048
NX = 1024
RECS = 32768
N_SUN = 2


def draw_heights(key, part):
    key = jax.random.fold_in(key, 11)
    first, second, third = jax.random.split(key, 3)
    standing = jax.random.randint(first, (NY, NX), 0, 100) < 5
    share = jax.random.uniform(second, (NY, NX), jnp.float32)
    tallness = 2.0 + 28.0 * share
    ground = 1.5 * jax.random.uniform(third, (NY, NX), jnp.float32)
    return (ground + jnp.where(standing, tallness, 0.0)).astype(jnp.float32)


def draw_sun_geometry(key, part):
    key = jax.random.fold_in(key, 12)
    keys = jax.random.split(key, 5)
    row_step = 2 * jax.random.randint(keys[0], (SUNS,), 0, 2) - 1
    col_step = jax.random.randint(keys[1], (SUNS,), -1, 2)
    rise = jax.random.randint(keys[2], (SUNS,), 1, min(10, MAXSTEP + 1))
    reach = jax.random.randint(keys[3], (SUNS,), 1, MAXSTEP + 1)
    longest = jax.random.randint(keys[4], (), 0, SUNS)
    reach = jnp.where(jnp.arange(SUNS) == longest, MAXSTEP, reach)
    return jnp.stack([row_step, col_step, rise, reach], axis=1).astype(jnp.int32)


def draw_sun_radiation(key, part):
    key = jax.random.fold_in(key, 13)
    share = jax.random.uniform(key, (SUNS, 3), jnp.float32)
    lower = jnp.array([100.0, 50.0, 300.0], jnp.float32)
    upper = jnp.array([900.0, 250.0, 420.0], jnp.float32)
    return (lower + share * (upper - lower)).astype(jnp.float32)


def touch_ends(entries, key, smallest, largest):
    dims = entries.shape
    place = [jax.random.randint(jax.random.fold_in(key, axis), (), 0, dims[axis]) for axis in range(len(dims))]
    entries = entries.at[tuple(place)].set(smallest)
    longest = dims.index(max(dims))
    place[longest] = (place[longest] + 1) % dims[longest]
    return entries.at[tuple(place)].set(largest)


def level_of(own_key, extent, shards, low, top_value):
    factor_of = 1.0
    for position, blocks in shards:
        draws = jax.random.uniform(jax.random.fold_in(jax.random.fold_in(own_key, 6), position), (blocks,), jnp.float32, low / len(shards), top_value / len(shards))
        factor_of = factor_of * jnp.repeat(jnp.exp(draws), extent[position] // blocks).reshape((-1,) + (1,) * (len(extent) - 1 - position))
    return factor_of


def shared_out(rng, own, number, rows, count, top, limit, lean):
    sequence = jax.random.permutation(rng, count)
    packed, usual = shares(count, rows * top, limit, lean, True), shares(count, rows * top, limit, lean, False)
    places = jnp.arange(count)

    def named(tallies, turn):
        used = int((tallies > 0).sum())
        fixed = max(1, used // 4)
        moved = fixed + (places - fixed + turn * (used - fixed)) % max(1, count - fixed)
        return jnp.zeros((count,), jnp.int32).at[sequence[jnp.where(places < fixed, places, moved)]].set(jnp.asarray(tallies, jnp.int32))

    tallies = jnp.where(number % 4 == 0, named(packed, number // 4), named(usual, number - number // 4 - 1))
    mixed = jax.random.permutation(jax.random.fold_in(own, 3), count)
    donor, receiver = mixed[0:count // 2 * 2:2], mixed[1:count // 2 * 2:2]
    margin = jnp.minimum(tallies[donor] - 1, limit - tallies[receiver]) // 2
    margin = jnp.where((donor == sequence[0]) | (receiver == sequence[0]) | (tallies[receiver] == 0), 0, jnp.maximum(margin, 0))
    moved = jax.random.randint(jax.random.fold_in(own, 4), (count // 2,), 0, 1 << 20) % (margin + 1)
    tallies = tallies.at[donor].add(-moved).at[receiver].add(moved)
    labels = jnp.searchsorted(jnp.cumsum(tallies), jnp.arange(rows * top), side="right").astype(jnp.int32)
    listing = labels.reshape(top, rows).T
    listing = listing[jax.random.permutation(jax.random.fold_in(own, 1), rows)]
    turn = jax.random.randint(jax.random.fold_in(own, 2), (rows, 1), 0, top)
    return jnp.take_along_axis(listing, (jnp.arange(top)[None, :] + turn) % top, axis=1)


def shares(number_of, total, bound, slope, full):
    portions = [(1 << 20) // math.isqrt(rank ** slope) + 1 for rank in range(1, number_of + 1)]
    largest = bound if full else min(bound, max(-(-total // number_of), total * portions[0] // sum(portions)))
    least = 1 if total - largest >= number_of - 1 else 0
    counts, surplus = [largest] + [least] * (number_of - 1), total - largest - least * (number_of - 1)
    while surplus > 0:
        free = [i for i in range(1, number_of) if counts[i] < largest] or [i for i in range(1, number_of) if counts[i] < bound]
        whole, budget = sum([portions[i] for i in free]), surplus
        for i in free:
            addition = min(bound - counts[i], max(1, budget * portions[i] // whole), surplus)
            counts[i] = counts[i] + addition
            surplus = surplus - addition
    return np.array(counts)


def gaussian(key, shape, scale, most, cuts=(), kind=jnp.bfloat16):
    values = scale * jax.random.normal(key, shape, jnp.float32)
    if cuts:
        values = values * level_of(key, shape, cuts, -0.22, 0.18)
    return jnp.clip(values, -most, most).astype(kind)


def setup_inputs(seed: int = 0) -> dict:
    streams_of = jax.random.split(jax.random.key(seed), 11)
    heights = draw_heights(jax.random.fold_in(streams_of[10], 71), 0)
    classes = touch_ends(jax.random.randint(streams_of[1], (NY, NX), 0, CLASSES), jax.random.fold_in(streams_of[1], 1), 0, CLASSES - 1).astype(jnp.int32)
    rate_table = jnp.clip(jax.random.uniform(streams_of[2], (2, CLASSES), jnp.float32, 0.03, 0.24), 0.03, 0.24)
    anomaly = gaussian(streams_of[3], (2, NY, NX), 4.0, 16.0, ((1, 16), (2, 2)), jnp.float32)
    view_coef = jnp.clip(0.099609375 + 0.7988281 * jax.random.uniform(streams_of[4], (3, NY, NX), jnp.float32) ** level_of(streams_of[4], (3, NY, NX), ((1, 16), (2, 2)), -0.2, 0.2), 0.099609375, 0.8984375).astype(jnp.bfloat16)
    sun_geometry = draw_sun_geometry(jax.random.fold_in(streams_of[10], 71), 0)
    sun_radiation = draw_sun_radiation(jax.random.fold_in(streams_of[10], 71), 0)
    record_tile_keys = jax.random.split(jax.random.fold_in(streams_of[7], 1), RECS // REC_DEV)
    record_tile_turns = jax.random.permutation(jax.random.fold_in(streams_of[7], 3), RECS // REC_DEV)
    record_tile = jax.vmap(lambda own, number: shared_out(jax.random.fold_in(streams_of[7], 2), own, number, REC_DEV, NTILE, 1, CAP, 2))(record_tile_keys, record_tile_turns).reshape((RECS, 1))
    record_cell = touch_ends(jax.random.randint(streams_of[8], (RECS,), 0, TR * NX), jax.random.fold_in(streams_of[8], 1), 0, (TR * NX) - 1).astype(jnp.int32)
    record_air = jnp.clip(20.0 + 15.0 * jax.random.uniform(streams_of[9], (RECS,), jnp.float32) ** level_of(streams_of[9], (RECS,), ((0, 32),), -0.2, 0.2), 20.0, 35.0)
    return dict(heights=heights, classes=classes, rate_table=rate_table, anomaly=anomaly, view_coef=view_coef, sun_geometry=sun_geometry, sun_radiation=sun_radiation, record_tile=record_tile, record_cell=record_cell, record_air=record_air)


SIGMA = 5.67e-08
BASE_KELVIN = 300.0
ZERO_CELSIUS = 273.15

def diffusion_rates(classes, rate_table):
    levels = jnp.arange(rate_table.shape[1], dtype=jnp.int32)
    onehot = (classes[None, :, :] == levels[:, None, None]).astype(jnp.float32)
    return jnp.einsum('gc,cij->gij', rate_table, onehot, precision=lax.Precision.HIGHEST)

def heat_update(padded, rate_field):
    centre = padded[:, 1:-1, 1:-1]
    beside_all = padded[:, :-2, 1:-1] + padded[:, 2:, 1:-1] + padded[:, 1:-1, :-2] + padded[:, 1:-1, 2:]
    return centre + rate_field * (beside_all - 4.0 * centre)

def sunlit_share(extended, row_count, col_count, geometry):
    centre = extended[MAXSTEP:MAXSTEP + row_count, MAXSTEP:MAXSTEP + col_count]
    rise = 0.1 * geometry[2].astype(jnp.float32)

    def mark_step(offset, depth):
        start_row = (MAXSTEP + geometry[0] * offset).astype(jnp.int32)
        start_col = (MAXSTEP + geometry[1] * offset).astype(jnp.int32)
        caster = lax.dynamic_slice(extended, (start_row, start_col), (row_count, col_count))
        excess = caster - centre - rise * offset.astype(jnp.float32)
        excess = jnp.where(offset <= geometry[3], excess, jnp.float32(-100.0))
        return jnp.maximum(depth, excess)
    depth = lax.fori_loop(1, MAXSTEP + 1, mark_step, jnp.full((row_count, col_count), -100.0, jnp.float32))
    return jnp.clip(0.5 - 0.5 * depth, 0.0, 1.0)

def radiant(sunlit, view_coef, surface, radiation):
    sky_view = view_coef[0].astype(jnp.float32)
    wall_view = view_coef[1].astype(jnp.float32)
    albedo = view_coef[2].astype(jnp.float32)
    direct = radiation[0]
    diffuse = radiation[1]
    sky_long = radiation[2]
    shortwave = 0.7 * (0.5 * direct * sunlit + diffuse * sky_view + (0.5 * direct + diffuse) * albedo * wall_view)
    ground_temp = BASE_KELVIN + surface[0]
    wall_temp = BASE_KELVIN + surface[1]
    ground_sq = ground_temp * ground_temp
    wall_sq = wall_temp * wall_temp
    longwave = 0.97 * (sky_view * sky_long + wall_view * SIGMA * wall_sq * wall_sq + (1.0 - sky_view) * SIGMA * ground_sq * ground_sq)
    absorbed = (shortwave + longwave) / (0.97 * SIGMA)
    return jnp.sqrt(jnp.sqrt(absorbed)) - ZERO_CELSIUS

def reference(heights, classes, rate_table, anomaly, view_coef, sun_geometry, sun_radiation, record_tile, record_cell, record_air):
    rate_field = diffusion_rates(classes, rate_table)
    surface = anomaly
    for section in range(HEAT_STEPS):
        padded = jnp.pad(surface, ((0, 0), (1, 1), (1, 1)))
        surface = heat_update(padded, rate_field)
    extended = jnp.pad(heights, MAXSTEP)

    def one_sun(pair):
        geometry, radiation = pair
        sunlit = sunlit_share(extended, NY, NX, geometry)
        return radiant(sunlit, view_coef, surface, radiation)
    radiant_temp = lax.map(one_sun, (sun_geometry, sun_radiation))
    sun_index = jnp.arange(RECS, dtype=jnp.int32) // REC_DEV % N_SUN
    target = record_tile[:, 0]
    row_index = target * TR + record_cell // NX
    col_index = record_cell % NX
    record_excess = radiant_temp[sun_index, row_index, col_index] - record_air
    return (radiant_temp, record_excess)
```

```python
import functools

import jax
import jax.numpy as jnp
from jax import lax
from jax.experimental import pallas as pl
from jax.experimental.pallas import tpu as pltpu
from jax.sharding import PartitionSpec as P

MAXSTEP = 24
HEAT_STEPS = 4
SIGMA = 5.67e-08
BASE_KELVIN = 300.0
ZERO_CELSIUS = 273.15
LANE = 128
VMEM_LIMIT = 50 * 2**20

VMEM = pl.BlockSpec(memory_space=pltpu.VMEM)
SMEM = pl.BlockSpec(memory_space=pltpu.SMEM)


def split3(x):
    hi = x.astype(jnp.bfloat16)
    rest = x - hi.astype(jnp.float32)
    mid = rest.astype(jnp.bfloat16)
    low = (rest - mid.astype(jnp.float32)).astype(jnp.bfloat16)
    return hi, mid, low


def dot(a, b, dims):
    return lax.dot_general(a, b, (dims, ((), ())), preferred_element_type=jnp.float32)


def rank_records(tile_ref, tiles):
    count = tile_ref.shape[1]
    levels = lax.broadcasted_iota(jnp.int32, (tiles, count), 0)
    lane = lax.broadcasted_iota(jnp.int32, (tiles, count), 1)
    named = levels == tile_ref[...]
    running = named.astype(jnp.int32)
    step = 1
    while step < count:
        running = running + jnp.where(lane >= step, pltpu.roll(running, step, 1), 0)
        step *= 2
    ranking = jnp.sum(jnp.where(named, running - 1, 0), axis=0, keepdims=True)
    return named, ranking


def bucket_kernel(tiles, capacity, tile_ref, cell_ref, cells_ref):
    named, ranking = rank_records(tile_ref, tiles)
    slots = lax.broadcasted_iota(jnp.int32, (capacity, tile_ref.shape[1]), 0)
    chosen = (slots == ranking).astype(jnp.float32).astype(jnp.bfloat16)
    cell = cell_ref[...]
    parts = [
        jnp.where(named, ((cell >> (8 * p)) & 255).astype(jnp.float32), 0.0) for p in range(3)
    ]
    placed = dot(jnp.concatenate(parts, 0).astype(jnp.bfloat16), chosen, ((1,), (1,)))
    low, mid, high = (placed[p * tiles : (p + 1) * tiles].astype(jnp.int32) for p in range(3))
    cells_ref[...] = low + mid * 256 + high * 65536


def heat_kernel(suns, table_ref, sun_ref, anomaly_ref, class_ref, rows_ref, side_ref, view_ref, base_ref):
    row_count, col_count = class_ref.shape

    def assemble(own, i):
        left = jnp.concatenate([own, rows_ref[i]], 0)
        return jnp.concatenate([left, side_ref[i]], 1)

    mark = assemble((class_ref[...] + 1).astype(jnp.float32), 2)
    rates = [jnp.zeros_like(mark), jnp.zeros_like(mark)]
    for level in range(table_ref.shape[1]):
        here = mark == float(level + 1)
        rates = [jnp.where(here, table_ref[g, level], rates[g]) for g in range(2)]
    fourth = []
    for g in range(2):
        value = assemble(anomaly_ref[g], g)
        high, wide = value.shape
        for _ in range(HEAT_STEPS):
            beside = (
                pltpu.roll(value, 1, 0)
                + pltpu.roll(value, high - 1, 0)
                + pltpu.roll(value, 1, 1)
                + pltpu.roll(value, wide - 1, 1)
            )
            value = value + rates[g] * (beside - 4.0 * value)
        temp = BASE_KELVIN + value[:row_count, :col_count]
        temp = temp * temp
        fourth.append(SIGMA * temp * temp)
    sky = view_ref[0].astype(jnp.float32)
    wall = view_ref[1].astype(jnp.float32)
    reflected = view_ref[2].astype(jnp.float32) * wall
    emitted = 0.97 * (wall * fourth[1] + (1.0 - sky) * fourth[0])
    for s in range(suns):
        direct, diffuse, sky_long = sun_ref[s, 0], sun_ref[s, 1], sun_ref[s, 2]
        base_ref[s] = (
            emitted
            + sky * (0.7 * diffuse + 0.97 * sky_long)
            + reflected * (0.7 * (0.5 * direct + diffuse))
        )


def sun_kernel(
    geometry_ref, sun_ref, heights_ref, base_ref, cells_ref, out_ref, sampled_ref, field, parts
):
    slabs, ext_rows, slab_cols = heights_ref.shape
    row_count = base_ref.shape[1]
    cols = slabs * slab_cols
    window = row_count + MAXSTEP
    chunks = cols // LANE
    row_step, col_step = geometry_ref[0, 0], geometry_ref[0, 1]
    slope = 0.1 * geometry_ref[0, 2].astype(jnp.float32)
    steps = jnp.minimum(geometry_ref[0, 3], MAXSTEP)
    forward = row_step > 0
    first = pl.multiple_of(jnp.where(forward, MAXSTEP, 0), 8)
    own = pl.multiple_of(jnp.where(forward, 0, MAXSTEP), 8)

    zero = jnp.zeros((field.shape[1], LANE), jnp.float32)
    for a in range(2):
        field[a, :, 0:LANE] = zero
        field[a, :, LANE + cols : 2 * LANE + cols] = zero
    for j in range(slabs):
        begin = LANE + j * slab_cols
        field[0, 8 : 8 + window, begin : begin + slab_cols] = heights_ref[j, pl.ds(first, window), :]

    def shifted(a, chunk, begin, length, distance):
        down, move = row_step * distance, col_step * distance
        sub = lax.broadcasted_iota(jnp.int32, (length, LANE), 0) & 7
        lane = lax.broadcasted_iota(jnp.int32, (length, LANE), 1)
        same_rows = (sub >= jnp.maximum(down, 0)) & (sub < 8 + jnp.minimum(down, 0))
        same_cols = (lane >= jnp.maximum(move, 0)) & (lane < LANE + jnp.minimum(move, 0))
        at = pl.multiple_of((chunk + 1) * LANE, LANE)
        beyond = pl.multiple_of((chunk + 1 + col_step) * LANE, LANE)

        def across(start):
            rows = pl.ds(pl.multiple_of(start, 8), length)
            here, there = field[a, rows, pl.ds(at, LANE)], field[a, rows, pl.ds(beyond, LANE)]
            return jnp.where(same_cols, here, there)

        whole = jnp.where(same_rows, across(begin), across(begin + 8 * row_step))
        whole = whole.reshape(length // 8, 8, LANE)
        whole = pltpu.roll(whole, (8 - down) & 7, 1)
        return pltpu.roll(whole.reshape(length, LANE), (LANE - move) & (LANE - 1), 1)

    reached = jnp.int32(1)
    a = 0
    for _ in range(5):
        distance = jnp.clip(steps - reached, 0, reached)

        def stage(chunk, carry, a=a, distance=distance):
            at = pl.multiple_of((chunk + 1) * LANE, LANE)
            ahead = shifted(a, chunk, 8, window, distance) - slope * distance.astype(jnp.float32)
            here = field[a, 8 : 8 + window, pl.ds(at, LANE)]
            field[1 - a, 8 : 8 + window, pl.ds(at, LANE)] = jnp.maximum(here, ahead)
            return carry

        lax.fori_loop(0, chunks, stage, 0)
        reached = reached + distance
        a = 1 - a

    half_direct = 0.35 * sun_ref[0, 0]
    per_slab = slab_cols // LANE

    for slab in range(slabs):

        def finish(k, carry, slab=slab):
            chunk = slab * per_slab + k
            lanes = pl.ds(pl.multiple_of(k * LANE, LANE), LANE)
            centre = heights_ref[slab, MAXSTEP : MAXSTEP + row_count, lanes]
            depth = shifted(a, chunk, 8 + own, row_count, 1) - slope - centre
            depth = jnp.where(steps >= 1, depth, -100.0)
            sunlit = jnp.clip(0.5 - 0.5 * depth, 0.0, 1.0)
            absorbed = (base_ref[slab, :, lanes] + half_direct * sunlit) * (1.0 / (0.97 * SIGMA))
            value = jnp.sqrt(jnp.sqrt(absorbed)) - ZERO_CELSIUS
            at = pl.multiple_of(chunk * LANE, LANE)
            out_ref[0, :, pl.ds(at, LANE)] = value
            for p, part in enumerate(split3(value.T)):
                parts[pl.ds(at, LANE), p * row_count : (p + 1) * row_count] = part
            return carry

        lax.fori_loop(0, per_slab, finish, 0)

    group = cells_ref.shape[1]
    block = 256
    row_iota = lax.broadcasted_iota(jnp.int32, (row_count, group), 0)
    col_iota = lax.broadcasted_iota(jnp.int32, (block, group), 0)
    for g in range(cells_ref.shape[0]):
        cell = cells_ref[g : g + 1, :]
        pick = (row_iota == cell // cols).astype(jnp.float32).astype(jnp.bfloat16)
        pick = jnp.concatenate([pick] * 3, 0)
        col = cell % cols

        def gather(b, total, pick=pick, col=col):
            at = pl.multiple_of(b * block, block)
            rows = dot(parts[pl.ds(at, block), :], pick, ((1,), (0,)))
            return total + jnp.where(col_iota == col - at, rows, 0.0)

        total = lax.fori_loop(0, cols // block, gather, jnp.zeros((block, group), jnp.float32), unroll=4)
        sampled_ref[g : g + 1, :] = jnp.sum(total, axis=0, keepdims=True)


def excess_kernel(tiles, tile_ref, returned_ref, air_ref, excess_ref):
    named, ranking = rank_records(tile_ref, tiles)
    capacity = returned_ref.shape[1]
    slots = lax.broadcasted_iota(jnp.int32, (capacity, tile_ref.shape[1]), 0)
    chosen = (slots == ranking).astype(jnp.float32).astype(jnp.bfloat16)
    spread = sum(dot(part, chosen, ((1,), (0,))) for part in split3(returned_ref[...]))
    value = jnp.sum(jnp.where(named, spread, 0.0), axis=0, keepdims=True)
    excess_ref[...] = value - air_ref[...]


def call(kernel, out_shape, in_specs, scratch_shapes=()):
    out_specs = jax.tree.map(lambda _: VMEM, out_shape)
    return pl.pallas_call(
        kernel,
        out_shape=out_shape,
        in_specs=in_specs,
        out_specs=out_specs,
        scratch_shapes=scratch_shapes,
        compiler_params=pltpu.CompilerParams(vmem_limit_bytes=VMEM_LIMIT),
    )


def f32(*shape):
    return jax.ShapeDtypeStruct(shape, jnp.float32)


def exchange(axis, last, initial):
    peers = lax.axis_size(axis)
    up = [(i, (i + 1) % peers) for i in range(peers - 1)]
    down = [(j, i) for i, j in up]
    return lax.ppermute(last, axis, up), lax.ppermute(initial, axis, down)


def on_device(
    heights,
    classes,
    rate_table,
    anomaly,
    view_coef,
    sun_geometry,
    sun_radiation,
    record_tile,
    record_cell,
    record_air,
):
    row_count, col_count = heights.shape
    suns, tiles = lax.axis_size("sun"), lax.axis_size("tile")
    records = record_cell.shape[0]
    cols = suns * col_count
    capacity = 2 * records // tiles
    w = HEAT_STEPS

    target = record_tile.reshape(1, records)
    cells = call(
        functools.partial(bucket_kernel, tiles, capacity),
        jax.ShapeDtypeStruct((tiles, capacity), jnp.int32),
        [VMEM, VMEM],
    )(target, record_cell.reshape(1, records))
    cells = lax.all_to_all(cells, "tile", split_axis=0, concat_axis=0, tiled=True)

    mark = (classes + 1).astype(jnp.float32)

    def edge(lo, hi, hlo, hhi):
        return jnp.concatenate(
            [anomaly[0, lo:hi], anomaly[1, lo:hi], mark[lo:hi], heights[hlo:hhi]], 0
        )

    before, after = exchange(
        "tile",
        edge(row_count - w, row_count, row_count - MAXSTEP, row_count),
        edge(0, w, 0, MAXSTEP),
    )
    rows = jnp.stack(
        [jnp.concatenate([after[i * w : (i + 1) * w], before[i * w : (i + 1) * w]], 0) for i in range(3)]
    )
    heights_ext = jnp.concatenate([before[3 * w :], heights, after[3 * w :]], 0)
    heights_all = lax.all_gather(heights_ext, "sun", axis=0)

    fields = jnp.concatenate([anomaly, mark[None]], 0)

    def column(lo, hi):
        return jnp.concatenate([fields[:, :, lo:hi], rows[:, :, lo:hi]], 1)

    left, right = exchange("sun", column(col_count - w, col_count), column(0, w))
    side = jnp.concatenate(
        [right, jnp.zeros((3, row_count + 2 * w, LANE - 2 * w), jnp.float32), left], 2
    )
    radiation_all = lax.all_gather(sun_radiation[0], "sun", axis=0)
    base = call(
        functools.partial(heat_kernel, suns),
        f32(suns, row_count, col_count),
        [SMEM, SMEM] + [VMEM] * 5,
    )(rate_table, radiation_all, anomaly, classes, rows, side, view_coef)
    base = lax.all_to_all(base, "sun", split_axis=0, concat_axis=0, tiled=True)

    group = 256
    window = row_count + MAXSTEP
    radiant_block, sampled = call(
        sun_kernel,
        (f32(1, row_count, cols), f32(tiles * capacity // group, group)),
        [SMEM, SMEM] + [VMEM] * 3,
        [
            pltpu.VMEM((2, window + 16, cols + 2 * LANE), jnp.float32),
            pltpu.VMEM((cols, 3 * row_count), jnp.bfloat16),
        ],
    )(sun_geometry, sun_radiation, heights_all, base, cells.reshape(-1, group))
    returned = lax.all_to_all(
        sampled.reshape(tiles, capacity), "tile", split_axis=0, concat_axis=0, tiled=True
    )
    excess = call(functools.partial(excess_kernel, tiles), f32(1, records), [VMEM] * 3)(
        target, returned, record_air.reshape(1, records)
    )
    return radiant_block, excess.reshape(records)


def solution(mesh):
    return jax.shard_map(
        on_device,
        mesh=mesh,
        in_specs=(
            P("tile", "sun"),
            P("tile", "sun"),
            P(),
            P(None, "tile", "sun"),
            P(None, "tile", "sun"),
            P("sun", None),
            P("sun", None),
            P(("tile", "sun"), None),
            P(("tile", "sun")),
            P(("tile", "sun")),
        ),
        out_specs=(P("sun", "tile", None), P(("tile", "sun"))),
        check_vma=False,
    )
```

```python
import functools

import jax
import jax.numpy as jnp
from jax import lax
from jax.experimental import pallas as pl
from jax.experimental.pallas import tpu as pltpu
from jax.sharding import PartitionSpec as P

MAXSTEP = 24
HEAT_STEPS = 4
SIGMA = 5.67e-08
BASE_KELVIN = 300.0
ZERO_CELSIUS = 273.15
LANE = 128
VMEM_LIMIT = 50 * 2**20

VMEM = pl.BlockSpec(memory_space=pltpu.VMEM)
SMEM = pl.BlockSpec(memory_space=pltpu.SMEM)


def split3(x):
    hi = x.astype(jnp.bfloat16)
    rest = x - hi.astype(jnp.float32)
    mid = rest.astype(jnp.bfloat16)
    low = (rest - mid.astype(jnp.float32)).astype(jnp.bfloat16)
    return hi, mid, low


def dot(a, b, dims):
    return lax.dot_general(a, b, (dims, ((), ())), preferred_element_type=jnp.float32)


def rank_records(tile_ref, tiles):
    count = tile_ref.shape[1]
    levels = lax.broadcasted_iota(jnp.int32, (tiles, count), 0)
    lane = lax.broadcasted_iota(jnp.int32, (tiles, count), 1)
    named = levels == tile_ref[...]
    running = named.astype(jnp.int32)
    step = 1
    while step < count:
        running = running + jnp.where(lane >= step, pltpu.roll(running, step, 1), 0)
        step *= 2
    ranking = jnp.sum(jnp.where(named, running - 1, 0), axis=0, keepdims=True)
    return named, ranking


def bucket(tiles, capacity, tile_ref, cell_ref):
    named, ranking = rank_records(tile_ref, tiles)
    slots = lax.broadcasted_iota(jnp.int32, (capacity, tile_ref.shape[1]), 0)
    chosen = (slots == ranking).astype(jnp.float32).astype(jnp.bfloat16)
    cell = cell_ref[...]
    pieces = [
        jnp.where(named, ((cell >> (8 * p)) & 255).astype(jnp.float32), 0.0) for p in range(3)
    ]
    placed = dot(jnp.concatenate(pieces, 0).astype(jnp.bfloat16), chosen, ((1,), (1,)))
    low, mid, high = (placed[p * tiles : (p + 1) * tiles].astype(jnp.int32) for p in range(3))
    return low + mid * 256 + high * 65536


def remote(src, dst, sems, k, tile, sun):
    return pltpu.make_async_remote_copy(
        src_ref=src,
        dst_ref=dst,
        send_sem=sems.at[0, k],
        recv_sem=sems.at[1, k],
        device_id=(tile, sun),
        device_id_type=pl.DeviceIdType.MESH,
    )


def greet(peers):
    barrier = pltpu.get_barrier_semaphore()
    for peer in peers:
        pl.semaphore_signal(
            barrier, inc=1, device_id=peer, device_id_type=pl.DeviceIdType.MESH
        )
    pl.semaphore_wait(barrier, len(peers))


def heat_kernel(
    tiles, suns, table_ref, sun_ref, heights_ref, anomaly_ref, class_ref, view_ref, tile_ref, cell_ref,
    heights_all, base_all, cells_in,
    fields, rows_in, cols_out, cols_in, corners_in, light_out, light_in, base_out, cells_out,
    near_sems, light_sems, cell_sems, height_sems, base_sems,
):
    row_count, col_count = class_ref.shape
    capacity = cells_in.shape[2]
    tile, sun = lax.axis_index("tile"), lax.axis_index("sun")
    above, below = lax.rem(tile + tiles - 1, tiles), lax.rem(tile + 1, tiles)
    before, after = lax.rem(sun + suns - 1, suns), lax.rem(sun + 1, suns)
    other_tiles = [lax.rem(tile + k, tiles) for k in range(1, tiles)]
    other_suns = [lax.rem(sun + k, suns) for k in range(1, suns)]

    fields[0] = anomaly_ref[0]
    fields[1] = anomaly_ref[1]
    fields[2] = (class_ref[...] + 1).astype(jnp.float32)
    last = col_count - LANE
    for i in range(3):
        cols_out[0, i] = fields[i, :, 0:LANE].T[0:8]
        cols_out[1, i] = fields[i, :, last:col_count].T[LANE - 8 : LANE]
    lane = lax.broadcasted_iota(jnp.int32, (1, LANE), 1)
    light = jnp.zeros((1, LANE), jnp.float32)
    for i in range(3):
        light = jnp.where(lane == i, sun_ref[0, i], light)
    light_out[...] = light
    light_in[sun] = light

    greet(
        [(t, sun) for t in other_tiles]
        + [(t, s) for s in other_suns for t in (above, tile, below)]
    )
    top, bottom = pl.ds(0, 8), pl.ds(row_count - 8, 8)
    first_cols, last_cols = pl.ds(0, LANE), pl.ds(last, LANE)
    near = [
        remote(cols_out.at[0], cols_in.at[1], near_sems, 0, tile, before),
        remote(cols_out.at[1], cols_in.at[0], near_sems, 1, tile, after),
        remote(fields.at[:, top, :], rows_in.at[0], near_sems, 2, above, sun),
        remote(fields.at[:, bottom, :], rows_in.at[1], near_sems, 3, below, sun),
        remote(fields.at[:, top, first_cols], corners_in.at[0, 1], near_sems, 4, above, before),
        remote(fields.at[:, top, last_cols], corners_in.at[0, 0], near_sems, 5, above, after),
        remote(fields.at[:, bottom, first_cols], corners_in.at[1, 1], near_sems, 6, below, before),
        remote(fields.at[:, bottom, last_cols], corners_in.at[1, 0], near_sems, 7, below, after),
    ] + [
        remote(light_out, light_in.at[sun], light_sems, k, tile, s)
        for k, s in enumerate(other_suns)
    ]
    for copy in near:
        copy.start()
    far = []
    for k, s in enumerate(other_suns):
        far.append(
            remote(heights_ref, heights_all.at[sun, pl.ds(MAXSTEP, row_count), :], height_sems, k, tile, s)
        )
    for k, s in enumerate([sun] + other_suns):
        at = suns - 1 + 2 * k
        far.append(
            remote(
                heights_ref.at[pl.ds(0, MAXSTEP), :],
                heights_all.at[sun, pl.ds(MAXSTEP + row_count, MAXSTEP), :],
                height_sems, at, above, s,
            )
        )
        far.append(
            remote(
                heights_ref.at[pl.ds(row_count - MAXSTEP, MAXSTEP), :],
                heights_all.at[sun, pl.ds(0, MAXSTEP), :],
                height_sems, at + 1, below, s,
            )
        )
    for copy in far:
        copy.start()
    heights_all[sun, MAXSTEP : MAXSTEP + row_count, :] = heights_ref[...]

    cells = bucket(tiles, capacity, tile_ref, cell_ref)
    for t in range(tiles):
        cells_out[t] = cells[t : t + 1]
    cells_in[tile] = cells_out[tile]
    for k, t in enumerate(other_tiles):
        copy = remote(cells_out.at[t], cells_in.at[tile], cell_sems, k, t, sun)
        copy.start()
        far.append(copy)

    for copy in near:
        copy.wait_recv()
    has_above, has_below = tile > 0, tile < tiles - 1
    has_before, has_after = sun > 0, sun < suns - 1
    wide = lax.broadcasted_iota(jnp.int32, (8, LANE), 1)

    def masked(condition, value):
        return jnp.where(condition, value, 0.0)

    def corner(k, i, present):
        left = masked(present & has_before, corners_in[k, 0, i])
        right = masked(present & has_after, corners_in[k, 1, i])
        return jnp.where(wide < LANE // 2, right, left)

    def assemble(i):
        own = jnp.concatenate(
            [fields[i], masked(has_below, rows_in[0, i]), masked(has_above, rows_in[1, i])], 0
        )
        flat = jnp.concatenate(
            [
                masked(has_after, cols_in[1, i]),
                jnp.zeros((LANE - 16, row_count), jnp.float32),
                masked(has_before, cols_in[0, i]),
            ],
            0,
        )
        side = jnp.concatenate([flat.T, corner(0, i, has_below), corner(1, i, has_above)], 0)
        return jnp.concatenate([own, side], 1)

    mark = assemble(2)
    rates = [jnp.zeros_like(mark), jnp.zeros_like(mark)]
    for level in range(table_ref.shape[1]):
        here = mark == float(level + 1)
        rates = [jnp.where(here, table_ref[g, level], rates[g]) for g in range(2)]
    fourth = []
    for g in range(2):
        value = assemble(g)
        high, broad = value.shape
        for _ in range(HEAT_STEPS):
            beside = (
                pltpu.roll(value, 1, 0)
                + pltpu.roll(value, high - 1, 0)
                + pltpu.roll(value, 1, 1)
                + pltpu.roll(value, broad - 1, 1)
            )
            value = value + rates[g] * (beside - 4.0 * value)
        temp = BASE_KELVIN + value[:row_count, :col_count]
        temp = temp * temp
        fourth.append(SIGMA * temp * temp)
    sky = view_ref[0].astype(jnp.float32)
    wall = view_ref[1].astype(jnp.float32)
    reflected = view_ref[2].astype(jnp.float32) * wall
    emitted = 0.97 * (wall * fourth[1] + (1.0 - sky) * fourth[0])
    for s in range(suns):
        received = light_in[s]
        direct, diffuse, sky_long = received[:, 0:1], received[:, 1:2], received[:, 2:3]
        base_out[s] = (
            emitted
            + sky * (0.7 * diffuse + 0.97 * sky_long)
            + reflected * (0.7 * (0.5 * direct + diffuse))
        )
    for k, s in enumerate(other_suns):
        copy = remote(base_out.at[s], base_all.at[sun], base_sems, k, tile, s)
        copy.start()
        far.append(copy)
    base_all[sun] = base_out[sun]
    for copy in far:
        copy.wait_recv()
    edge = jnp.zeros((suns, MAXSTEP, col_count), jnp.float32)

    @pl.when(tile == 0)
    def _():
        heights_all[:, 0:MAXSTEP, :] = edge

    @pl.when(tile == tiles - 1)
    def _():
        heights_all[:, MAXSTEP + row_count : 2 * MAXSTEP + row_count, :] = edge

    for copy in near + far:
        copy.wait_send()


def sun_kernel(
    geometry_ref, sun_ref, heights_ref, base_ref, cells_ref, out_ref, sampled_ref, field, parts
):
    slabs, ext_rows, slab_cols = heights_ref.shape
    row_count = base_ref.shape[1]
    cols = slabs * slab_cols
    window = row_count + MAXSTEP
    chunks = cols // LANE
    row_step, col_step = geometry_ref[0, 0], geometry_ref[0, 1]
    slope = 0.1 * geometry_ref[0, 2].astype(jnp.float32)
    steps = jnp.minimum(geometry_ref[0, 3], MAXSTEP)
    forward = row_step > 0
    first = pl.multiple_of(jnp.where(forward, MAXSTEP, 0), 8)
    own = pl.multiple_of(jnp.where(forward, 0, MAXSTEP), 8)

    zero = jnp.zeros((field.shape[1], LANE), jnp.float32)
    for a in range(2):
        field[a, :, 0:LANE] = zero
        field[a, :, LANE + cols : 2 * LANE + cols] = zero
    for j in range(slabs):
        begin = LANE + j * slab_cols
        field[0, 8 : 8 + window, begin : begin + slab_cols] = heights_ref[j, pl.ds(first, window), :]

    def shifted(a, chunk, begin, length, distance):
        down, move = row_step * distance, col_step * distance
        sub = lax.broadcasted_iota(jnp.int32, (length, LANE), 0) & 7
        lane = lax.broadcasted_iota(jnp.int32, (length, LANE), 1)
        same_rows = (sub >= jnp.maximum(down, 0)) & (sub < 8 + jnp.minimum(down, 0))
        same_cols = (lane >= jnp.maximum(move, 0)) & (lane < LANE + jnp.minimum(move, 0))
        at = pl.multiple_of((chunk + 1) * LANE, LANE)
        beyond = pl.multiple_of((chunk + 1 + col_step) * LANE, LANE)

        def across(start):
            rows = pl.ds(pl.multiple_of(start, 8), length)
            here, there = field[a, rows, pl.ds(at, LANE)], field[a, rows, pl.ds(beyond, LANE)]
            return jnp.where(same_cols, here, there)

        whole = jnp.where(same_rows, across(begin), across(begin + 8 * row_step))
        whole = whole.reshape(length // 8, 8, LANE)
        whole = pltpu.roll(whole, (8 - down) & 7, 1)
        return pltpu.roll(whole.reshape(length, LANE), (LANE - move) & (LANE - 1), 1)

    reached = jnp.int32(1)
    a = 0
    for _ in range(5):
        distance = jnp.clip(steps - reached, 0, reached)

        def stage(chunk, carry, a=a, distance=distance):
            at = pl.multiple_of((chunk + 1) * LANE, LANE)
            ahead = shifted(a, chunk, 8, window, distance) - slope * distance.astype(jnp.float32)
            here = field[a, 8 : 8 + window, pl.ds(at, LANE)]
            field[1 - a, 8 : 8 + window, pl.ds(at, LANE)] = jnp.maximum(here, ahead)
            return carry

        lax.fori_loop(0, chunks, stage, 0)
        reached = reached + distance
        a = 1 - a

    half_direct = 0.35 * sun_ref[0, 0]
    per_slab = slab_cols // LANE

    for slab in range(slabs):

        def finish(k, carry, slab=slab):
            chunk = slab * per_slab + k
            lanes = pl.ds(pl.multiple_of(k * LANE, LANE), LANE)
            centre = heights_ref[slab, MAXSTEP : MAXSTEP + row_count, lanes]
            depth = shifted(a, chunk, 8 + own, row_count, 1) - slope - centre
            depth = jnp.where(steps >= 1, depth, -100.0)
            sunlit = jnp.clip(0.5 - 0.5 * depth, 0.0, 1.0)
            absorbed = (base_ref[slab, :, lanes] + half_direct * sunlit) * (1.0 / (0.97 * SIGMA))
            value = jnp.sqrt(jnp.sqrt(absorbed)) - ZERO_CELSIUS
            at = pl.multiple_of(chunk * LANE, LANE)
            out_ref[0, :, pl.ds(at, LANE)] = value
            for p, part in enumerate(split3(value.T)):
                parts[pl.ds(at, LANE), p * row_count : (p + 1) * row_count] = part
            return carry

        lax.fori_loop(0, per_slab, finish, 0)

    capacity = cells_ref.shape[2]
    group = 2 * capacity
    block = 256
    row_iota = lax.broadcasted_iota(jnp.int32, (row_count, group), 0)
    col_iota = lax.broadcasted_iota(jnp.int32, (block, group), 0)
    for g in range(cells_ref.shape[0] // 2):
        cell = jnp.concatenate([cells_ref[2 * g], cells_ref[2 * g + 1]], 1)
        pick = (row_iota == cell // cols).astype(jnp.float32).astype(jnp.bfloat16)
        pick = jnp.concatenate([pick] * 3, 0)
        col = cell % cols

        def gather(b, total, pick=pick, col=col):
            at = pl.multiple_of(b * block, block)
            rows = dot(parts[pl.ds(at, block), :], pick, ((1,), (0,)))
            return total + jnp.where(col_iota == col - at, rows, 0.0)

        total = lax.fori_loop(0, cols // block, gather, jnp.zeros((block, group), jnp.float32), unroll=4)
        total = jnp.sum(total, axis=0, keepdims=True)
        sampled_ref[2 * g] = total[:, :capacity]
        sampled_ref[2 * g + 1] = total[:, capacity:]


def excess_kernel(tiles, suns, tile_ref, sampled_ref, air_ref, excess_ref, returned, sems):
    tile, sun = lax.axis_index("tile"), lax.axis_index("sun")
    others = [lax.rem(tile + k, tiles) for k in range(1, tiles)]
    greet([(t, sun) for t in others])
    copies = [
        remote(sampled_ref.at[t], returned.at[tile], sems, k, t, sun) for k, t in enumerate(others)
    ]
    for copy in copies:
        copy.start()
    returned[tile] = sampled_ref[tile]
    named, ranking = rank_records(tile_ref, tiles)
    capacity = returned.shape[2]
    slots = lax.broadcasted_iota(jnp.int32, (capacity, tile_ref.shape[1]), 0)
    chosen = (slots == ranking).astype(jnp.float32).astype(jnp.bfloat16)
    for copy in copies:
        copy.wait()
    values = jnp.concatenate([returned[t] for t in range(tiles)], 0)
    spread = sum(dot(part, chosen, ((1,), (0,))) for part in split3(values))
    value = jnp.sum(jnp.where(named, spread, 0.0), axis=0, keepdims=True)
    excess_ref[...] = value - air_ref[...]


def call(kernel, out_shape, in_specs, scratch_shapes=(), collective_id=None):
    out_specs = jax.tree.map(lambda _: VMEM, out_shape)
    sends = collective_id is not None
    return pl.pallas_call(
        kernel,
        out_shape=out_shape,
        in_specs=in_specs,
        out_specs=out_specs,
        scratch_shapes=scratch_shapes,
        compiler_params=pltpu.CompilerParams(
            vmem_limit_bytes=VMEM_LIMIT, collective_id=collective_id, has_side_effects=sends
        ),
    )


def f32(*shape):
    return jax.ShapeDtypeStruct(shape, jnp.float32)


def on_device(
    heights,
    classes,
    rate_table,
    anomaly,
    view_coef,
    sun_geometry,
    sun_radiation,
    record_tile,
    record_cell,
    record_air,
):
    row_count, col_count = heights.shape
    suns, tiles = lax.axis_size("sun"), lax.axis_size("tile")
    records = record_cell.shape[0]
    cols = suns * col_count
    capacity = -(-2 * records // tiles // LANE) * LANE
    window = row_count + MAXSTEP
    target = record_tile.reshape(1, records)

    def room(*shape):
        return pltpu.VMEM(shape, jnp.float32)

    def sems(count):
        return pltpu.SemaphoreType.DMA((2, count))

    heights_all, base, cells = call(
        functools.partial(heat_kernel, tiles, suns),
        (
            f32(suns, window + MAXSTEP, col_count),
            f32(suns, row_count, col_count),
            jax.ShapeDtypeStruct((tiles, 1, capacity), jnp.int32),
        ),
        [SMEM, SMEM] + [VMEM] * 6,
        [
            room(3, row_count, col_count),
            room(2, 3, 8, col_count),
            room(2, 3, 8, row_count),
            room(2, 3, 8, row_count),
            room(2, 2, 3, 8, LANE),
            room(1, LANE),
            room(suns, 1, LANE),
            room(suns, row_count, col_count),
            pltpu.VMEM((tiles, 1, capacity), jnp.int32),
            sems(8),
            sems(suns - 1),
            sems(tiles - 1),
            sems(3 * suns - 1),
            sems(suns - 1),
        ],
        0,
    )(
        rate_table,
        sun_radiation,
        heights,
        anomaly,
        classes,
        view_coef,
        target,
        record_cell.reshape(1, records),
    )
    radiant_block, sampled = call(
        sun_kernel,
        (f32(1, row_count, cols), f32(tiles, 1, capacity)),
        [SMEM, SMEM] + [VMEM] * 3,
        [
            room(2, window + 16, cols + 2 * LANE),
            pltpu.VMEM((cols, 3 * row_count), jnp.bfloat16),
        ],
    )(sun_geometry, sun_radiation, heights_all, base, cells)
    excess = call(
        functools.partial(excess_kernel, tiles, suns),
        f32(1, records),
        [VMEM] * 3,
        [room(tiles, 1, capacity), sems(tiles - 1)],
        1,
    )(target, sampled, record_air.reshape(1, records))
    return radiant_block, excess.reshape(records)


def solution(mesh):
    return jax.shard_map(
        on_device,
        mesh=mesh,
        in_specs=(
            P("tile", "sun"),
            P("tile", "sun"),
            P(),
            P(None, "tile", "sun"),
            P(None, "tile", "sun"),
            P("sun", None),
            P("sun", None),
            P(("tile", "sun"), None),
            P(("tile", "sun")),
            P(("tile", "sun")),
        ),
        out_specs=(P("sun", "tile", None), P(("tile", "sun"))),
        check_vma=False,
    )
```

```python
import functools

import jax
import jax.numpy as jnp
from jax import lax
from jax.experimental import pallas as pl
from jax.experimental.pallas import tpu as pltpu
from jax.sharding import PartitionSpec as P

MAXSTEP = 24
HEAT_STEPS = 4
SIGMA = 5.67e-08
BASE_KELVIN = 300.0
ZERO_CELSIUS = 273.15
LANE = 128
VMEM_LIMIT = 50 * 2**20

VMEM = pl.BlockSpec(memory_space=pltpu.VMEM)
SMEM = pl.BlockSpec(memory_space=pltpu.SMEM)


def split3(x):
    hi = x.astype(jnp.bfloat16)
    rest = x - hi.astype(jnp.float32)
    mid = rest.astype(jnp.bfloat16)
    low = (rest - mid.astype(jnp.float32)).astype(jnp.bfloat16)
    return hi, mid, low


def dot(a, b, dims):
    return lax.dot_general(a, b, (dims, ((), ())), preferred_element_type=jnp.float32)


def rank_records(tile_ref, tiles):
    count = tile_ref.shape[1]
    levels = lax.broadcasted_iota(jnp.int32, (tiles, count), 0)
    lane = lax.broadcasted_iota(jnp.int32, (tiles, count), 1)
    named = levels == tile_ref[...]
    running = named.astype(jnp.int32)
    step = 1
    while step < count:
        running = running + jnp.where(lane >= step, pltpu.roll(running, step, 1), 0)
        step *= 2
    ranking = jnp.sum(jnp.where(named, running - 1, 0), axis=0, keepdims=True)
    return named, ranking


def bucket(tiles, capacity, tile_ref, cell_ref):
    named, ranking = rank_records(tile_ref, tiles)
    slots = lax.broadcasted_iota(jnp.int32, (capacity, tile_ref.shape[1]), 0)
    chosen = (slots == ranking).astype(jnp.float32).astype(jnp.bfloat16)
    cell = cell_ref[...]
    pieces = [
        jnp.where(named, ((cell >> (8 * p)) & 255).astype(jnp.float32), 0.0) for p in range(3)
    ]
    placed = dot(jnp.concatenate(pieces, 0).astype(jnp.bfloat16), chosen, ((1,), (1,)))
    low, mid, high = (placed[p * tiles : (p + 1) * tiles].astype(jnp.int32) for p in range(3))
    return low + mid * 256 + high * 65536


def remote(src, dst, sems, k, tile, sun):
    return pltpu.make_async_remote_copy(
        src_ref=src,
        dst_ref=dst,
        send_sem=sems.at[0, k],
        recv_sem=sems.at[1, k],
        device_id=(tile, sun),
        device_id_type=pl.DeviceIdType.MESH,
    )


def greet(peers):
    barrier = pltpu.get_barrier_semaphore()
    for peer in peers:
        pl.semaphore_signal(
            barrier, inc=1, device_id=peer, device_id_type=pl.DeviceIdType.MESH
        )
    return lambda: pl.semaphore_wait(barrier, len(peers))


def heat_kernel(
    tiles, suns, table_ref, sun_ref, heights_ref, anomaly_hbm, class_hbm, view_hbm, tile_hbm, cell_hbm,
    heights_all, base_all, cells_in,
    fields, rows_in, cols_out, cols_in, corners_in, light_out, light_in, base_out, cells_out,
    class_ref, view_ref, tile_ref, cell_ref,
    near_sems, light_sems, cell_sems, height_sems, base_sems, load_sems,
):
    row_count, col_count = class_ref.shape
    capacity = cells_in.shape[2]
    tile, sun = lax.axis_index("tile"), lax.axis_index("sun")
    above, below = lax.rem(tile + tiles - 1, tiles), lax.rem(tile + 1, tiles)
    before, after = lax.rem(sun + suns - 1, suns), lax.rem(sun + 1, suns)
    other_tiles = [lax.rem(tile + k, tiles) for k in range(1, tiles)]
    other_suns = [lax.rem(sun + k, suns) for k in range(1, suns)]

    wait_peers = greet(
        [(t, sun) for t in other_tiles]
        + [(t, s) for s in other_suns for t in (above, tile, below)]
    )
    loads = [
        pltpu.make_async_copy(src, dst, load_sems.at[k])
        for k, (src, dst) in enumerate(
            [
                (class_hbm, class_ref),
                (anomaly_hbm, fields.at[pl.ds(0, 2)]),
                (tile_hbm, tile_ref),
                (cell_hbm, cell_ref),
                (view_hbm, view_ref),
                (heights_ref, heights_all.at[sun, pl.ds(MAXSTEP, row_count), :]),
            ]
        )
    ]
    for load in loads:
        load.start()
    loads[0].wait()
    loads[1].wait()
    fields[2] = (class_ref[...] + 1).astype(jnp.float32)
    last = col_count - LANE
    for i in range(3):
        cols_out[0, i] = fields[i, :, 0:LANE].T[0:8]
        cols_out[1, i] = fields[i, :, last:col_count].T[LANE - 8 : LANE]
    lane = lax.broadcasted_iota(jnp.int32, (1, LANE), 1)
    light = jnp.zeros((1, LANE), jnp.float32)
    for i in range(3):
        light = jnp.where(lane == i, sun_ref[0, i], light)
    light_out[...] = light
    light_in[sun] = light

    wait_peers()
    top, bottom = pl.ds(0, 8), pl.ds(row_count - 8, 8)
    first_cols, last_cols = pl.ds(0, LANE), pl.ds(last, LANE)
    near = [
        remote(cols_out.at[0], cols_in.at[1], near_sems, 0, tile, before),
        remote(cols_out.at[1], cols_in.at[0], near_sems, 1, tile, after),
        remote(fields.at[:, top, :], rows_in.at[0], near_sems, 2, above, sun),
        remote(fields.at[:, bottom, :], rows_in.at[1], near_sems, 3, below, sun),
        remote(fields.at[:, top, first_cols], corners_in.at[0, 1], near_sems, 4, above, before),
        remote(fields.at[:, top, last_cols], corners_in.at[0, 0], near_sems, 5, above, after),
        remote(fields.at[:, bottom, first_cols], corners_in.at[1, 1], near_sems, 6, below, before),
        remote(fields.at[:, bottom, last_cols], corners_in.at[1, 0], near_sems, 7, below, after),
    ] + [
        remote(light_out, light_in.at[sun], light_sems, k, tile, s)
        for k, s in enumerate(other_suns)
    ]
    for copy in near:
        copy.start()
    far = []
    for k, s in enumerate(other_suns):
        far.append(
            remote(heights_ref, heights_all.at[sun, pl.ds(MAXSTEP, row_count), :], height_sems, k, tile, s)
        )
    for k, s in enumerate([sun] + other_suns):
        at = suns - 1 + 2 * k
        far.append(
            remote(
                heights_ref.at[pl.ds(0, MAXSTEP), :],
                heights_all.at[sun, pl.ds(MAXSTEP + row_count, MAXSTEP), :],
                height_sems, at, above, s,
            )
        )
        far.append(
            remote(
                heights_ref.at[pl.ds(row_count - MAXSTEP, MAXSTEP), :],
                heights_all.at[sun, pl.ds(0, MAXSTEP), :],
                height_sems, at + 1, below, s,
            )
        )
    for copy in far:
        copy.start()
    for load in loads[2:]:
        load.wait()
    cells = bucket(tiles, capacity, tile_ref, cell_ref)
    for t in range(tiles):
        cells_out[t] = cells[t : t + 1]
    cells_in[tile] = cells_out[tile]
    for k, t in enumerate(other_tiles):
        copy = remote(cells_out.at[t], cells_in.at[tile], cell_sems, k, t, sun)
        copy.start()
        far.append(copy)

    for copy in near:
        copy.wait_recv()
    has_above, has_below = tile > 0, tile < tiles - 1
    has_before, has_after = sun > 0, sun < suns - 1
    wide = lax.broadcasted_iota(jnp.int32, (8, LANE), 1)

    def masked(condition, value):
        return jnp.where(condition, value, 0.0)

    def corner(k, i, present):
        left = masked(present & has_before, corners_in[k, 0, i])
        right = masked(present & has_after, corners_in[k, 1, i])
        return jnp.where(wide < LANE // 2, right, left)

    def assemble(i):
        own = jnp.concatenate(
            [fields[i], masked(has_below, rows_in[0, i]), masked(has_above, rows_in[1, i])], 0
        )
        flat = jnp.concatenate(
            [
                masked(has_after, cols_in[1, i]),
                jnp.zeros((LANE - 16, row_count), jnp.float32),
                masked(has_before, cols_in[0, i]),
            ],
            0,
        )
        side = jnp.concatenate([flat.T, corner(0, i, has_below), corner(1, i, has_above)], 0)
        return jnp.concatenate([own, side], 1)

    mark = assemble(2)
    rates = [jnp.zeros_like(mark), jnp.zeros_like(mark)]
    for level in range(table_ref.shape[1]):
        here = mark == float(level + 1)
        rates = [jnp.where(here, table_ref[g, level], rates[g]) for g in range(2)]
    fourth = []
    for g in range(2):
        value = assemble(g)
        high, broad = value.shape
        for _ in range(HEAT_STEPS):
            beside = (
                pltpu.roll(value, 1, 0)
                + pltpu.roll(value, high - 1, 0)
                + pltpu.roll(value, 1, 1)
                + pltpu.roll(value, broad - 1, 1)
            )
            value = value + rates[g] * (beside - 4.0 * value)
        temp = BASE_KELVIN + value[:row_count, :col_count]
        temp = temp * temp
        fourth.append(SIGMA * temp * temp)
    sky = view_ref[0].astype(jnp.float32)
    wall = view_ref[1].astype(jnp.float32)
    reflected = view_ref[2].astype(jnp.float32) * wall
    emitted = 0.97 * (wall * fourth[1] + (1.0 - sky) * fourth[0])
    for s in range(suns):
        received = light_in[s]
        direct, diffuse, sky_long = received[:, 0:1], received[:, 1:2], received[:, 2:3]
        base_out[s] = (
            emitted
            + sky * (0.7 * diffuse + 0.97 * sky_long)
            + reflected * (0.7 * (0.5 * direct + diffuse))
        )
    for k, s in enumerate(other_suns):
        copy = remote(base_out.at[s], base_all.at[sun], base_sems, k, tile, s)
        copy.start()
        far.append(copy)
    base_all[sun] = base_out[sun]
    for copy in far:
        copy.wait_recv()
    edge = jnp.zeros((suns, MAXSTEP, col_count), jnp.float32)

    @pl.when(tile == 0)
    def _():
        heights_all[:, 0:MAXSTEP, :] = edge

    @pl.when(tile == tiles - 1)
    def _():
        heights_all[:, MAXSTEP + row_count : 2 * MAXSTEP + row_count, :] = edge

    for copy in near + far:
        copy.wait_send()


def sun_kernel(
    geometry_ref, sun_ref, heights_ref, base_ref, cells_ref, out_ref, sampled_ref, field, parts
):
    slabs, ext_rows, slab_cols = heights_ref.shape
    row_count = base_ref.shape[1]
    cols = slabs * slab_cols
    window = row_count + MAXSTEP
    chunks = cols // LANE
    row_step, col_step = geometry_ref[0, 0], geometry_ref[0, 1]
    slope = 0.1 * geometry_ref[0, 2].astype(jnp.float32)
    steps = jnp.minimum(geometry_ref[0, 3], MAXSTEP)
    forward = row_step > 0
    first = pl.multiple_of(jnp.where(forward, MAXSTEP, 0), 8)
    own = pl.multiple_of(jnp.where(forward, 0, MAXSTEP), 8)

    zero = jnp.zeros((field.shape[1], LANE), jnp.float32)
    for a in range(2):
        field[a, :, 0:LANE] = zero
        field[a, :, LANE + cols : 2 * LANE + cols] = zero
    for j in range(slabs):
        begin = LANE + j * slab_cols
        field[0, 8 : 8 + window, begin : begin + slab_cols] = heights_ref[j, pl.ds(first, window), :]

    def shifted(a, chunk, begin, length, distance):
        down, move = row_step * distance, col_step * distance
        sub = lax.broadcasted_iota(jnp.int32, (length, LANE), 0) & 7
        lane = lax.broadcasted_iota(jnp.int32, (length, LANE), 1)
        same_rows = (sub >= jnp.maximum(down, 0)) & (sub < 8 + jnp.minimum(down, 0))
        same_cols = (lane >= jnp.maximum(move, 0)) & (lane < LANE + jnp.minimum(move, 0))
        at = pl.multiple_of((chunk + 1) * LANE, LANE)
        beyond = pl.multiple_of((chunk + 1 + col_step) * LANE, LANE)

        def across(start):
            rows = pl.ds(pl.multiple_of(start, 8), length)
            here, there = field[a, rows, pl.ds(at, LANE)], field[a, rows, pl.ds(beyond, LANE)]
            return jnp.where(same_cols, here, there)

        whole = jnp.where(same_rows, across(begin), across(begin + 8 * row_step))
        whole = whole.reshape(length // 8, 8, LANE)
        whole = pltpu.roll(whole, (8 - down) & 7, 1)
        return pltpu.roll(whole.reshape(length, LANE), (LANE - move) & (LANE - 1), 1)

    reached = jnp.int32(1)
    a = 0
    for _ in range(5):
        distance = jnp.clip(steps - reached, 0, reached)

        def stage(chunk, carry, a=a, distance=distance):
            at = pl.multiple_of((chunk + 1) * LANE, LANE)
            ahead = shifted(a, chunk, 8, window, distance) - slope * distance.astype(jnp.float32)
            here = field[a, 8 : 8 + window, pl.ds(at, LANE)]
            field[1 - a, 8 : 8 + window, pl.ds(at, LANE)] = jnp.maximum(here, ahead)
            return carry

        lax.fori_loop(0, chunks, stage, 0)
        reached = reached + distance
        a = 1 - a

    half_direct = 0.35 * sun_ref[0, 0]
    per_slab = slab_cols // LANE

    for slab in range(slabs):

        def finish(k, carry, slab=slab):
            chunk = slab * per_slab + k
            lanes = pl.ds(pl.multiple_of(k * LANE, LANE), LANE)
            centre = heights_ref[slab, MAXSTEP : MAXSTEP + row_count, lanes]
            depth = shifted(a, chunk, 8 + own, row_count, 1) - slope - centre
            depth = jnp.where(steps >= 1, depth, -100.0)
            sunlit = jnp.clip(0.5 - 0.5 * depth, 0.0, 1.0)
            absorbed = (base_ref[slab, :, lanes] + half_direct * sunlit) * (1.0 / (0.97 * SIGMA))
            value = jnp.sqrt(jnp.sqrt(absorbed)) - ZERO_CELSIUS
            at = pl.multiple_of(chunk * LANE, LANE)
            out_ref[0, :, pl.ds(at, LANE)] = value
            for p, part in enumerate(split3(value.T)):
                parts[pl.ds(at, LANE), p * row_count : (p + 1) * row_count] = part
            return carry

        lax.fori_loop(0, per_slab, finish, 0)

    capacity = cells_ref.shape[2]
    group = 2 * capacity
    block = 256
    row_iota = lax.broadcasted_iota(jnp.int32, (row_count, group), 0)
    col_iota = lax.broadcasted_iota(jnp.int32, (block, group), 0)
    for g in range(cells_ref.shape[0] // 2):
        cell = jnp.concatenate([cells_ref[2 * g], cells_ref[2 * g + 1]], 1)
        pick = (row_iota == cell // cols).astype(jnp.float32).astype(jnp.bfloat16)
        pick = jnp.concatenate([pick] * 3, 0)
        col = cell % cols

        def gather(b, total, pick=pick, col=col):
            at = pl.multiple_of(b * block, block)
            rows = dot(parts[pl.ds(at, block), :], pick, ((1,), (0,)))
            return total + jnp.where(col_iota == col - at, rows, 0.0)

        total = lax.fori_loop(0, cols // block, gather, jnp.zeros((block, group), jnp.float32), unroll=4)
        total = jnp.sum(total, axis=0, keepdims=True)
        sampled_ref[2 * g] = total[:, :capacity]
        sampled_ref[2 * g + 1] = total[:, capacity:]


def excess_kernel(tiles, suns, tile_ref, sampled_ref, air_ref, excess_ref, returned, sems):
    tile, sun = lax.axis_index("tile"), lax.axis_index("sun")
    others = [lax.rem(tile + k, tiles) for k in range(1, tiles)]
    greet([(t, sun) for t in others])()
    copies = [
        remote(sampled_ref.at[t], returned.at[tile], sems, k, t, sun) for k, t in enumerate(others)
    ]
    for copy in copies:
        copy.start()
    returned[tile] = sampled_ref[tile]
    named, ranking = rank_records(tile_ref, tiles)
    capacity = returned.shape[2]
    slots = lax.broadcasted_iota(jnp.int32, (capacity, tile_ref.shape[1]), 0)
    chosen = (slots == ranking).astype(jnp.float32).astype(jnp.bfloat16)
    for copy in copies:
        copy.wait()
    values = jnp.concatenate([returned[t] for t in range(tiles)], 0)
    spread = sum(dot(part, chosen, ((1,), (0,))) for part in split3(values))
    value = jnp.sum(jnp.where(named, spread, 0.0), axis=0, keepdims=True)
    excess_ref[...] = value - air_ref[...]


def call(kernel, out_shape, in_specs, scratch_shapes=(), collective_id=None):
    out_specs = jax.tree.map(lambda _: VMEM, out_shape)
    sends = collective_id is not None
    return pl.pallas_call(
        kernel,
        out_shape=out_shape,
        in_specs=in_specs,
        out_specs=out_specs,
        scratch_shapes=scratch_shapes,
        compiler_params=pltpu.CompilerParams(
            vmem_limit_bytes=VMEM_LIMIT, collective_id=collective_id, has_side_effects=sends
        ),
    )


def f32(*shape):
    return jax.ShapeDtypeStruct(shape, jnp.float32)


def on_device(
    heights,
    classes,
    rate_table,
    anomaly,
    view_coef,
    sun_geometry,
    sun_radiation,
    record_tile,
    record_cell,
    record_air,
):
    row_count, col_count = heights.shape
    suns, tiles = lax.axis_size("sun"), lax.axis_size("tile")
    records = record_cell.shape[0]
    cols = suns * col_count
    capacity = -(-2 * records // tiles // LANE) * LANE
    window = row_count + MAXSTEP
    target = record_tile.reshape(1, records)

    def room(*shape):
        return pltpu.VMEM(shape, jnp.float32)

    def sems(count):
        return pltpu.SemaphoreType.DMA((2, count))

    heights_all, base, cells = call(
        functools.partial(heat_kernel, tiles, suns),
        (
            f32(suns, window + MAXSTEP, col_count),
            f32(suns, row_count, col_count),
            jax.ShapeDtypeStruct((tiles, 1, capacity), jnp.int32),
        ),
        [SMEM, SMEM] + [pl.BlockSpec(memory_space=pl.ANY)] * 6,
        [
            room(3, row_count, col_count),
            room(2, 3, 8, col_count),
            room(2, 3, 8, row_count),
            room(2, 3, 8, row_count),
            room(2, 2, 3, 8, LANE),
            room(1, LANE),
            room(suns, 1, LANE),
            room(suns, row_count, col_count),
            pltpu.VMEM((tiles, 1, capacity), jnp.int32),
            pltpu.VMEM(classes.shape, jnp.int32),
            pltpu.VMEM(view_coef.shape, view_coef.dtype),
            pltpu.VMEM((1, records), jnp.int32),
            pltpu.VMEM((1, records), jnp.int32),
            sems(8),
            sems(suns - 1),
            sems(tiles - 1),
            sems(3 * suns - 1),
            sems(suns - 1),
            pltpu.SemaphoreType.DMA((6,)),
        ],
        0,
    )(
        rate_table,
        sun_radiation,
        heights,
        anomaly,
        classes,
        view_coef,
        target,
        record_cell.reshape(1, records),
    )
    radiant_block, sampled = call(
        sun_kernel,
        (f32(1, row_count, cols), f32(tiles, 1, capacity)),
        [SMEM, SMEM] + [VMEM] * 3,
        [
            room(2, window + 16, cols + 2 * LANE),
            pltpu.VMEM((cols, 3 * row_count), jnp.bfloat16),
        ],
    )(sun_geometry, sun_radiation, heights_all, base, cells)
    excess = call(
        functools.partial(excess_kernel, tiles, suns),
        f32(1, records),
        [VMEM] * 3,
        [room(tiles, 1, capacity), sems(tiles - 1)],
        1,
    )(target, sampled, record_air.reshape(1, records))
    return radiant_block, excess.reshape(records)


def solution(mesh):
    return jax.shard_map(
        on_device,
        mesh=mesh,
        in_specs=(
            P("tile", "sun"),
            P("tile", "sun"),
            P(),
            P(None, "tile", "sun"),
            P(None, "tile", "sun"),
            P("sun", None),
            P("sun", None),
            P(("tile", "sun"), None),
            P(("tile", "sun")),
            P(("tile", "sun")),
        ),
        out_specs=(P("sun", "tile", None), P(("tile", "sun"))),
        check_vma=False,
    )
```

```python
import functools

import jax
import jax.numpy as jnp
from jax import lax
from jax.experimental import pallas as pl
from jax.experimental.pallas import tpu as pltpu
from jax.sharding import PartitionSpec as P

MAXSTEP = 24
HEAT_STEPS = 4
SIGMA = 5.67e-08
BASE_KELVIN = 300.0
ZERO_CELSIUS = 273.15
LANE = 128
VMEM_LIMIT = 64 * 2**20

VMEM = pl.BlockSpec(memory_space=pltpu.VMEM)
SMEM = pl.BlockSpec(memory_space=pltpu.SMEM)


def split3(x):
    hi = x.astype(jnp.bfloat16)
    rest = x - hi.astype(jnp.float32)
    mid = rest.astype(jnp.bfloat16)
    low = (rest - mid.astype(jnp.float32)).astype(jnp.bfloat16)
    return hi, mid, low


def dot(a, b, dims):
    return lax.dot_general(a, b, (dims, ((), ())), preferred_element_type=jnp.float32)


def rank_records(tile_ref, tiles):
    count = tile_ref.shape[1]
    levels = lax.broadcasted_iota(jnp.int32, (tiles, count), 0)
    lane = lax.broadcasted_iota(jnp.int32, (tiles, count), 1)
    named = levels == tile_ref[...]
    running = named.astype(jnp.int32)
    step = 1
    while step < count:
        running = running + jnp.where(lane >= step, pltpu.roll(running, step, 1), 0)
        step *= 2
    ranking = jnp.sum(jnp.where(named, running - 1, 0), axis=0, keepdims=True)
    return named, ranking


def bucket(tiles, capacity, tile_ref, cell_ref):
    named, ranking = rank_records(tile_ref, tiles)
    slots = lax.broadcasted_iota(jnp.int32, (capacity, tile_ref.shape[1]), 0)
    chosen = (slots == ranking).astype(jnp.float32).astype(jnp.bfloat16)
    cell = cell_ref[...]
    pieces = [
        jnp.where(named, ((cell >> (8 * p)) & 255).astype(jnp.float32), 0.0) for p in range(3)
    ]
    placed = dot(jnp.concatenate(pieces, 0).astype(jnp.bfloat16), chosen, ((1,), (1,)))
    low, mid, high = (placed[p * tiles : (p + 1) * tiles].astype(jnp.int32) for p in range(3))
    return low + mid * 256 + high * 65536


def remote(src, dst, sems, k, tile, sun):
    return pltpu.make_async_remote_copy(
        src_ref=src,
        dst_ref=dst,
        send_sem=sems.at[0, k],
        recv_sem=sems.at[1, k],
        device_id=(tile, sun),
        device_id_type=pl.DeviceIdType.MESH,
    )


def greet(peers):
    barrier = pltpu.get_barrier_semaphore()
    for peer in peers:
        pl.semaphore_signal(
            barrier, inc=1, device_id=peer, device_id_type=pl.DeviceIdType.MESH
        )
    return lambda: pl.semaphore_wait(barrier, len(peers))


def heat_kernel(
    tiles, suns, table_ref, sun_ref, heights_ref, anomaly_hbm, class_hbm, view_hbm, tile_hbm, cell_hbm,
    heights_all, base_all, cells_in,
    fields, rows_in, cols_out, cols_in, corners_in, light_out, light_in, base_out, cells_out,
    class_ref, view_ref, tile_ref, cell_ref,
    near_sems, light_sems, cell_sems, height_sems, base_sems, load_sems,
):
    row_count, col_count = class_ref.shape
    capacity = cells_in.shape[2]
    tile, sun = lax.axis_index("tile"), lax.axis_index("sun")
    above, below = lax.rem(tile + tiles - 1, tiles), lax.rem(tile + 1, tiles)
    before, after = lax.rem(sun + suns - 1, suns), lax.rem(sun + 1, suns)
    other_tiles = [lax.rem(tile + k, tiles) for k in range(1, tiles)]
    other_suns = [lax.rem(sun + k, suns) for k in range(1, suns)]

    wait_peers = greet(
        [(t, sun) for t in other_tiles]
        + [(t, s) for s in other_suns for t in (above, tile, below)]
    )
    loads = [
        pltpu.make_async_copy(src, dst, load_sems.at[k])
        for k, (src, dst) in enumerate(
            [
                (class_hbm, class_ref),
                (anomaly_hbm, fields.at[pl.ds(0, 2)]),
                (tile_hbm, tile_ref),
                (cell_hbm, cell_ref),
                (view_hbm, view_ref),
                (heights_ref, heights_all.at[sun, pl.ds(MAXSTEP, row_count), :]),
            ]
        )
    ]
    for load in loads:
        load.start()
    loads[0].wait()
    loads[1].wait()
    fields[2] = (class_ref[...] + 1).astype(jnp.float32)
    last = col_count - LANE
    for i in range(3):
        cols_out[0, i] = fields[i, :, 0:LANE].T[0:8]
        cols_out[1, i] = fields[i, :, last:col_count].T[LANE - 8 : LANE]
    lane = lax.broadcasted_iota(jnp.int32, (1, LANE), 1)
    light = jnp.zeros((1, LANE), jnp.float32)
    for i in range(3):
        light = jnp.where(lane == i, sun_ref[0, i], light)
    light_out[...] = light
    light_in[sun] = light

    wait_peers()
    top, bottom = pl.ds(0, 8), pl.ds(row_count - 8, 8)
    first_cols, last_cols = pl.ds(0, LANE), pl.ds(last, LANE)
    near = [
        remote(cols_out.at[0], cols_in.at[1], near_sems, 0, tile, before),
        remote(cols_out.at[1], cols_in.at[0], near_sems, 1, tile, after),
        remote(fields.at[:, top, :], rows_in.at[0], near_sems, 2, above, sun),
        remote(fields.at[:, bottom, :], rows_in.at[1], near_sems, 3, below, sun),
        remote(fields.at[:, top, first_cols], corners_in.at[0, 1], near_sems, 4, above, before),
        remote(fields.at[:, top, last_cols], corners_in.at[0, 0], near_sems, 5, above, after),
        remote(fields.at[:, bottom, first_cols], corners_in.at[1, 1], near_sems, 6, below, before),
        remote(fields.at[:, bottom, last_cols], corners_in.at[1, 0], near_sems, 7, below, after),
    ] + [
        remote(light_out, light_in.at[sun], light_sems, k, tile, s)
        for k, s in enumerate(other_suns)
    ]
    for copy in near:
        copy.start()
    far = []
    for k, s in enumerate(other_suns):
        far.append(
            remote(heights_ref, heights_all.at[sun, pl.ds(MAXSTEP, row_count), :], height_sems, k, tile, s)
        )
    for k, s in enumerate([sun] + other_suns):
        at = suns - 1 + 2 * k
        far.append(
            remote(
                heights_ref.at[pl.ds(0, MAXSTEP), :],
                heights_all.at[sun, pl.ds(MAXSTEP + row_count, MAXSTEP), :],
                height_sems, at, above, s,
            )
        )
        far.append(
            remote(
                heights_ref.at[pl.ds(row_count - MAXSTEP, MAXSTEP), :],
                heights_all.at[sun, pl.ds(0, MAXSTEP), :],
                height_sems, at + 1, below, s,
            )
        )
    for copy in far:
        copy.start()
    for load in loads[2:]:
        load.wait()
    cells = bucket(tiles, capacity, tile_ref, cell_ref)
    for t in range(tiles):
        cells_out[t] = cells[t : t + 1]
    cells_in[tile] = cells_out[tile]
    for k, t in enumerate(other_tiles):
        copy = remote(cells_out.at[t], cells_in.at[tile], cell_sems, k, t, sun)
        copy.start()
        far.append(copy)

    for copy in near:
        copy.wait_recv()
    has_above, has_below = tile > 0, tile < tiles - 1
    has_before, has_after = sun > 0, sun < suns - 1
    wide = lax.broadcasted_iota(jnp.int32, (8, LANE), 1)

    def masked(condition, value):
        return jnp.where(condition, value, 0.0)

    def corner(k, i, present):
        left = masked(present & has_before, corners_in[k, 0, i])
        right = masked(present & has_after, corners_in[k, 1, i])
        return jnp.where(wide < LANE // 2, right, left)

    def assemble(i):
        own = jnp.concatenate(
            [fields[i], masked(has_below, rows_in[0, i]), masked(has_above, rows_in[1, i])], 0
        )
        flat = jnp.concatenate(
            [
                masked(has_after, cols_in[1, i]),
                jnp.zeros((LANE - 16, row_count), jnp.float32),
                masked(has_before, cols_in[0, i]),
            ],
            0,
        )
        side = jnp.concatenate([flat.T, corner(0, i, has_below), corner(1, i, has_above)], 0)
        return jnp.concatenate([own, side], 1)

    mark = assemble(2)
    rates = [jnp.zeros_like(mark), jnp.zeros_like(mark)]
    for level in range(table_ref.shape[1]):
        here = mark == float(level + 1)
        rates = [jnp.where(here, table_ref[g, level], rates[g]) for g in range(2)]
    fourth = []
    for g in range(2):
        value = assemble(g)
        high, broad = value.shape
        for _ in range(HEAT_STEPS):
            beside = (
                pltpu.roll(value, 1, 0)
                + pltpu.roll(value, high - 1, 0)
                + pltpu.roll(value, 1, 1)
                + pltpu.roll(value, broad - 1, 1)
            )
            value = value + rates[g] * (beside - 4.0 * value)
        temp = BASE_KELVIN + value[:row_count, :col_count]
        temp = temp * temp
        fourth.append(SIGMA * temp * temp)
    sky = view_ref[0].astype(jnp.float32)
    wall = view_ref[1].astype(jnp.float32)
    reflected = view_ref[2].astype(jnp.float32) * wall
    emitted = 0.97 * (wall * fourth[1] + (1.0 - sky) * fourth[0])
    for s in range(suns):
        received = light_in[s]
        direct, diffuse, sky_long = received[:, 0:1], received[:, 1:2], received[:, 2:3]
        base_out[s] = (
            emitted
            + sky * (0.7 * diffuse + 0.97 * sky_long)
            + reflected * (0.7 * (0.5 * direct + diffuse))
        )
    for k, s in enumerate(other_suns):
        copy = remote(base_out.at[s], base_all.at[sun], base_sems, k, tile, s)
        copy.start()
        far.append(copy)
    base_all[sun] = base_out[sun]
    for copy in far:
        copy.wait_recv()
    edge = jnp.zeros((suns, MAXSTEP, col_count), jnp.float32)

    @pl.when(tile == 0)
    def _():
        heights_all[:, 0:MAXSTEP, :] = edge

    @pl.when(tile == tiles - 1)
    def _():
        heights_all[:, MAXSTEP + row_count : 2 * MAXSTEP + row_count, :] = edge

    for copy in near + far:
        copy.wait_send()


def sun_kernel(
    geometry_ref, sun_ref, heights_ref, base_ref, cells_ref, out_ref, sampled_ref, field, parts
):
    slabs, ext_rows, slab_cols = heights_ref.shape
    row_count = base_ref.shape[1]
    cols = slabs * slab_cols
    window = row_count + MAXSTEP
    chunks = cols // LANE
    row_step, col_step = geometry_ref[0, 0], geometry_ref[0, 1]
    slope = 0.1 * geometry_ref[0, 2].astype(jnp.float32)
    steps = jnp.minimum(geometry_ref[0, 3], MAXSTEP)
    forward = row_step > 0
    first = pl.multiple_of(jnp.where(forward, MAXSTEP, 0), 8)
    own = pl.multiple_of(jnp.where(forward, 0, MAXSTEP), 8)

    zero = jnp.zeros((field.shape[1], LANE), jnp.float32)
    for a in range(2):
        field[a, :, 0:LANE] = zero
        field[a, :, LANE + cols : 2 * LANE + cols] = zero
    for j in range(slabs):
        begin = LANE + j * slab_cols
        field[0, 8 : 8 + window, begin : begin + slab_cols] = heights_ref[j, pl.ds(first, window), :]

    def shifted(a, chunk, begin, length, distance):
        down, move = row_step * distance, col_step * distance
        sub = lax.broadcasted_iota(jnp.int32, (length, LANE), 0) & 7
        lane = lax.broadcasted_iota(jnp.int32, (length, LANE), 1)
        same_rows = (sub >= jnp.maximum(down, 0)) & (sub < 8 + jnp.minimum(down, 0))
        same_cols = (lane >= jnp.maximum(move, 0)) & (lane < LANE + jnp.minimum(move, 0))
        at = pl.multiple_of((chunk + 1) * LANE, LANE)
        beyond = pl.multiple_of((chunk + 1 + col_step) * LANE, LANE)

        def across(start):
            rows = pl.ds(pl.multiple_of(start, 8), length)
            here, there = field[a, rows, pl.ds(at, LANE)], field[a, rows, pl.ds(beyond, LANE)]
            return jnp.where(same_cols, here, there)

        whole = jnp.where(same_rows, across(begin), across(begin + 8 * row_step))
        whole = whole.reshape(length // 8, 8, LANE)
        whole = pltpu.roll(whole, (8 - down) & 7, 1)
        return pltpu.roll(whole.reshape(length, LANE), (LANE - move) & (LANE - 1), 1)

    reached = jnp.int32(1)
    a = 0
    for _ in range(5):
        distance = jnp.clip(steps - reached, 0, reached)

        def stage(chunk, carry, a=a, distance=distance):
            at = pl.multiple_of((chunk + 1) * LANE, LANE)
            ahead = shifted(a, chunk, 8, window, distance) - slope * distance.astype(jnp.float32)
            here = field[a, 8 : 8 + window, pl.ds(at, LANE)]
            field[1 - a, 8 : 8 + window, pl.ds(at, LANE)] = jnp.maximum(here, ahead)
            return carry

        lax.fori_loop(0, chunks, stage, 0)
        reached = reached + distance
        a = 1 - a

    half_direct = 0.35 * sun_ref[0, 0]
    per_slab = slab_cols // LANE

    for slab in range(slabs):

        def finish(k, carry, slab=slab):
            chunk = slab * per_slab + k
            lanes = pl.ds(pl.multiple_of(k * LANE, LANE), LANE)
            centre = heights_ref[slab, MAXSTEP : MAXSTEP + row_count, lanes]
            depth = shifted(a, chunk, 8 + own, row_count, 1) - slope - centre
            depth = jnp.where(steps >= 1, depth, -100.0)
            sunlit = jnp.clip(0.5 - 0.5 * depth, 0.0, 1.0)
            absorbed = (base_ref[slab, :, lanes] + half_direct * sunlit) * (1.0 / (0.97 * SIGMA))
            value = jnp.sqrt(jnp.sqrt(absorbed)) - ZERO_CELSIUS
            at = pl.multiple_of(chunk * LANE, LANE)
            out_ref[0, :, pl.ds(at, LANE)] = value
            for p, part in enumerate(split3(value.T)):
                parts[pl.ds(at, LANE), p * row_count : (p + 1) * row_count] = part
            return carry

        lax.fori_loop(0, per_slab, finish, 0)

    capacity = cells_ref.shape[2]
    group = 2 * capacity
    block = 256
    row_iota = lax.broadcasted_iota(jnp.int32, (row_count, group), 0)
    col_iota = lax.broadcasted_iota(jnp.int32, (block, group), 0)
    for g in range(cells_ref.shape[0] // 2):
        cell = jnp.concatenate([cells_ref[2 * g], cells_ref[2 * g + 1]], 1)
        pick = (row_iota == cell // cols).astype(jnp.float32).astype(jnp.bfloat16)
        pick = jnp.concatenate([pick] * 3, 0)
        col = cell % cols

        def gather(b, total, pick=pick, col=col):
            at = pl.multiple_of(b * block, block)
            rows = dot(parts[pl.ds(at, block), :], pick, ((1,), (0,)))
            return total + jnp.where(col_iota == col - at, rows, 0.0)

        total = lax.fori_loop(0, cols // block, gather, jnp.zeros((block, group), jnp.float32), unroll=4)
        total = jnp.sum(total, axis=0, keepdims=True)
        sampled_ref[2 * g] = total[:, :capacity]
        sampled_ref[2 * g + 1] = total[:, capacity:]


def excess_kernel(tiles, suns, tile_ref, sampled_ref, air_ref, excess_ref, returned, sems):
    tile, sun = lax.axis_index("tile"), lax.axis_index("sun")
    others = [lax.rem(tile + k, tiles) for k in range(1, tiles)]
    greet([(t, sun) for t in others])()
    copies = [
        remote(sampled_ref.at[t], returned.at[tile], sems, k, t, sun) for k, t in enumerate(others)
    ]
    for copy in copies:
        copy.start()
    returned[tile] = sampled_ref[tile]
    named, ranking = rank_records(tile_ref, tiles)
    capacity = returned.shape[2]
    slots = lax.broadcasted_iota(jnp.int32, (capacity, tile_ref.shape[1]), 0)
    chosen = (slots == ranking).astype(jnp.float32).astype(jnp.bfloat16)
    for copy in copies:
        copy.wait()
    values = jnp.concatenate([returned[t] for t in range(tiles)], 0)
    spread = sum(dot(part, chosen, ((1,), (0,))) for part in split3(values))
    value = jnp.sum(jnp.where(named, spread, 0.0), axis=0, keepdims=True)
    excess_ref[...] = value - air_ref[...]


def call(kernel, out_shape, in_specs, scratch_shapes=(), collective_id=None):
    out_specs = jax.tree.map(lambda _: VMEM, out_shape)
    sends = collective_id is not None
    return pl.pallas_call(
        kernel,
        out_shape=out_shape,
        in_specs=in_specs,
        out_specs=out_specs,
        scratch_shapes=scratch_shapes,
        compiler_params=pltpu.CompilerParams(
            vmem_limit_bytes=VMEM_LIMIT, collective_id=collective_id, has_side_effects=sends
        ),
    )


def f32(*shape):
    return jax.ShapeDtypeStruct(shape, jnp.float32)


def on_device(
    heights,
    classes,
    rate_table,
    anomaly,
    view_coef,
    sun_geometry,
    sun_radiation,
    record_tile,
    record_cell,
    record_air,
):
    row_count, col_count = heights.shape
    suns, tiles = lax.axis_size("sun"), lax.axis_size("tile")
    records = record_cell.shape[0]
    cols = suns * col_count
    capacity = -(-2 * records // tiles // LANE) * LANE
    window = row_count + MAXSTEP
    target = record_tile.reshape(1, records)

    def room(*shape):
        return pltpu.VMEM(shape, jnp.float32)

    def sems(count):
        return pltpu.SemaphoreType.DMA((2, count))

    heights_all, base, cells = call(
        functools.partial(heat_kernel, tiles, suns),
        (
            f32(suns, window + MAXSTEP, col_count),
            f32(suns, row_count, col_count),
            jax.ShapeDtypeStruct((tiles, 1, capacity), jnp.int32),
        ),
        [SMEM, SMEM] + [pl.BlockSpec(memory_space=pltpu.HBM)] * 6,
        [
            room(3, row_count, col_count),
            room(2, 3, 8, col_count),
            room(2, 3, 8, row_count),
            room(2, 3, 8, row_count),
            room(2, 2, 3, 8, LANE),
            room(1, LANE),
            room(suns, 1, LANE),
            room(suns, row_count, col_count),
            pltpu.VMEM((tiles, 1, capacity), jnp.int32),
            pltpu.VMEM(classes.shape, jnp.int32),
            pltpu.VMEM(view_coef.shape, view_coef.dtype),
            pltpu.VMEM((1, records), jnp.int32),
            pltpu.VMEM((1, records), jnp.int32),
            sems(8),
            sems(suns - 1),
            sems(tiles - 1),
            sems(3 * suns - 1),
            sems(suns - 1),
            pltpu.SemaphoreType.DMA((6,)),
        ],
        0,
    )(
        rate_table,
        sun_radiation,
        heights,
        anomaly,
        classes,
        view_coef,
        target,
        record_cell.reshape(1, records),
    )
    radiant_block, sampled = call(
        sun_kernel,
        (f32(1, row_count, cols), f32(tiles, 1, capacity)),
        [SMEM, SMEM] + [VMEM] * 3,
        [
            room(2, window + 16, cols + 2 * LANE),
            pltpu.VMEM((cols, 3 * row_count), jnp.bfloat16),
        ],
    )(sun_geometry, sun_radiation, heights_all, base, cells)
    excess = call(
        functools.partial(excess_kernel, tiles, suns),
        f32(1, records),
        [VMEM] * 3,
        [room(tiles, 1, capacity), sems(tiles - 1)],
        1,
    )(target, sampled, record_air.reshape(1, records))
    return radiant_block, excess.reshape(records)


def solution(mesh):
    return jax.shard_map(
        on_device,
        mesh=mesh,
        in_specs=(
            P("tile", "sun"),
            P("tile", "sun"),
            P(),
            P(None, "tile", "sun"),
            P(None, "tile", "sun"),
            P("sun", None),
            P("sun", None),
            P(("tile", "sun"), None),
            P(("tile", "sun")),
            P(("tile", "sun")),
        ),
        out_specs=(P("sun", "tile", None), P(("tile", "sun"))),
        check_vma=False,
    )
```
